256 devices in a mesh: inst: 32 (over y, x, z_lo), tp: 8 (over z_hi, core).
Axes of the slice: x: 4, y: 4, z: 8 (z_hi: 4, z_lo: 2; z = z_hi * 2 + z_lo), core: 2. Of those that a mesh axis runs over, the one named last changes fastest.
Arguments:
- queries: bfloat16 [2, 2048, 8192], P(None, 'inst', 'tp'), may hold values from -6 to 6
- new_kv: bfloat16 [2, 2, 2048, 1024], P(None, None, 'inst', 'tp'), may hold values from -6 to 6
- kv_pages: bfloat16 [32768, 2, 16, 1024], P('inst', None, None, 'tp'), may hold values from -6 to 6
- block_tables: int32 [2048, 16], P('inst'), may hold values from 0 to 1023, as said below
- lengths: int32 [2048], P('inst'), may hold values from 1 to 256, as said below
- migrating: int32 [64], P('inst'), may hold values from 0 to 63, as said below
- partner: int32 [32], replicated, may hold values from 0 to 31, as said below
- out_weight: bfloat16 [8192, 4096], P('tp'), may hold values from -0.0625 to 0.0625
Outputs:
- attended: bfloat16 [2, 2048, 4096], P(None, 'inst', 'tp')
The draws below stay inside these ranges and needn't reach their ends.
Inputs may be any that keep to these rules, and one draw needn't show every extreme that they name: `block_tables`: the rows of one instance hold each of its 1024 page numbers once. `lengths`: every instance has a request of exactly 256 tokens. `migrating`: the 2 slots of one instance differ. partner[partner[i]] = i and partner[i] != i; some instance i is paired with i + 1.
All inputs are finite; a program needn't handle non-finite values.
Results may differ from the reference program's by a relative error of at most 0.015.
Values may be sent and summed in bfloat16 or wider, within the bound.
No kernel may reach another device: no remote copies, remote signals or barrier semaphores. Data moves between devices by JAX's collectives and lax.ppermute only.
A program may use at most 128 MiB of HBM per device.

```python
import jax
import jax.numpy as jnp
from jax import lax

H = 64
KVH = 8
HD = 128
DW = 4096
REQ = 64
MIG = 2
PAGE = 16
MAXP = 16
STEPS = 2
PAGES = 1024
N_INST = 32


def draw_queries(key, part):
    key = jax.random.fold_in(key, 21)
    first = jax.random.fold_in(key, 0)
    shape = (STEPS, N_INST * REQ, H, HD)
    drawn = jnp.clip(jax.random.normal(first, shape, jnp.float32), -6.0, 6.0)
    return drawn.reshape(STEPS, N_INST * REQ, H * HD).astype(jnp.bfloat16)


def draw_kv_pages(key, part):
    key = jax.random.fold_in(key, 22)
    first = jax.random.fold_in(key, 0)
    shape = (N_INST * PAGES, 2, PAGE, KVH, HD)
    drawn = jnp.clip(jax.random.normal(first, shape, jnp.float32), -6.0, 6.0)
    return drawn.reshape(N_INST * PAGES, 2, PAGE, KVH * HD).astype(jnp.bfloat16)


def draw_block_tables(key, part):
    key = jax.random.fold_in(key, 11)
    keys = jax.random.split(key, N_INST)
    perms = jax.vmap(lambda k: jax.random.permutation(k, PAGES))(keys)
    return perms.reshape(N_INST * REQ, MAXP).astype(jnp.int32)


def draw_lengths(key, part):
    key = jax.random.fold_in(key, 12)
    first, second = jax.random.split(key)
    drawn = jax.random.randint(first, (N_INST, REQ), 1, MAXP * PAGE + 1)
    longest = jax.random.randint(second, (N_INST, 1), 0, REQ)
    slots = jnp.arange(REQ, dtype=jnp.int32)[None, :]
    drawn = jnp.where(slots == longest, MAXP * PAGE, drawn)
    return drawn.reshape(N_INST * REQ).astype(jnp.int32)


def draw_migrating(key, part):
    key = jax.random.fold_in(key, 13)
    keys = jax.random.split(key, N_INST)
    perms = jax.vmap(lambda k: jax.random.permutation(k, REQ)[:MIG])(keys)
    return perms.reshape(N_INST * MIG).astype(jnp.int32)


def draw_partner(key, part):
    key = jax.random.fold_in(key, 14)
    first, second = jax.random.split(key)
    ranks = jax.random.permutation(first, N_INST).astype(jnp.int32)
    lower = jax.random.randint(second, (), 0, N_INST - 1).astype(jnp.int32)
    ids = jnp.arange(N_INST, dtype=jnp.int32)
    scores = jnp.where(ids == lower, -2, jnp.where(ids == lower + 1, -1, ranks))
    order = jnp.argsort(scores, stable=True).astype(jnp.int32)
    evens = order[0::2]
    odds = order[1::2]
    paired = jnp.zeros((N_INST,), jnp.int32)
    paired = paired.at[evens].set(odds)
    paired = paired.at[odds].set(evens)
    return paired


def shard_levels(stream_key, extent, pieces, least, largest):
    def one(axis_at, parts):
        draws = jax.random.uniform(jax.random.fold_in(jax.random.fold_in(stream_key, 6), axis_at), (parts,), jnp.float32, least / len(pieces), largest / len(pieces))
        return jnp.repeat(jnp.exp(draws), extent[axis_at] // parts).reshape((-1,) + (1,) * (len(extent) - axis_at - 1))

    loudness = one(*pieces[0])
    for cut in pieces[1:]:
        loudness = loudness * one(*cut)
    return loudness


def gaussian(own_key, shape, scale, reach, pieces=(), held_as=jnp.bfloat16):
    level = shard_levels(own_key, shape, pieces, -0.22, 0.18) if pieces else 1.0
    values = jax.random.normal(own_key, shape, jnp.float32) * scale * level
    return jnp.minimum(jnp.maximum(values, -reach), reach).astype(held_as)


def setup_inputs(seed: int = 0) -> dict:
    key_list = jax.random.split(jax.random.key(seed), 9)
    queries = draw_queries(jax.random.fold_in(key_list[8], 71), 0)
    new_kv = gaussian(key_list[1], (STEPS, 2, N_INST * REQ, KVH * HD), 1.0, 6.0, ((2, 32), (3, 8)))
    kv_pages = draw_kv_pages(jax.random.fold_in(key_list[8], 71), 0)
    block_tables = draw_block_tables(jax.random.fold_in(key_list[8], 71), 0)
    lengths = draw_lengths(jax.random.fold_in(key_list[8], 71), 0)
    migrating = draw_migrating(jax.random.fold_in(key_list[8], 71), 0)
    partner = draw_partner(jax.random.fold_in(key_list[8], 71), 0)
    out_weight = gaussian(key_list[7], (H * HD, DW), (H * HD) ** -0.5, 0.0625, ((0, 8),))
    return {"queries": queries, "new_kv": new_kv, "kv_pages": kv_pages, "block_tables": block_tables, "lengths": lengths, "migrating": migrating, "partner": partner, "out_weight": out_weight}


def reference(queries, new_kv, kv_pages, block_tables, lengths, migrating, partner, out_weight):
    width = KVH * HD
    group = H // KVH
    span = MAXP * PAGE
    pages = kv_pages.reshape(N_INST, PAGES, 2, PAGE, width)
    tables = block_tables.reshape(N_INST, REQ, MAXP)
    counts = lengths.reshape(N_INST, REQ)
    moving = migrating.reshape(N_INST, MIG)
    base = jnp.arange(N_INST, dtype=jnp.int32)
    src_inst = jnp.broadcast_to(base[:, None], (N_INST, REQ))
    src_slot = jnp.broadcast_to(jnp.arange(REQ, dtype=jnp.int32)[None, :], (N_INST, REQ))
    row_ids = jnp.broadcast_to(base[:, None], (N_INST, MIG))
    src_inst = src_inst.at[row_ids, moving].set(jnp.broadcast_to(partner[:, None], (N_INST, MIG)).astype(jnp.int32))
    src_slot = src_slot.at[row_ids, moving].set(moving[partner].astype(jnp.int32))
    query_all = queries.reshape(STEPS, N_INST, REQ, KVH, group, HD)
    fresh_all = new_kv.reshape(STEPS, 2, N_INST, REQ, KVH, HD)
    scale = 1.0 / (HD ** 0.5)

    def one(inst):
        s_inst = src_inst[inst]
        s_slot = src_slot[inst]
        index = tables[s_inst, s_slot]
        blocks = pages[s_inst[:, None], index]
        keys = blocks[:, :, 0].reshape(REQ, span, KVH, HD).astype(jnp.float32)
        values = blocks[:, :, 1].reshape(REQ, span, KVH, HD).astype(jnp.float32)
        valid = jnp.arange(span, dtype=jnp.int32)[None, :] < counts[s_inst, s_slot][:, None]
        results = []
        for step in range(STEPS):
            query = query_all[step, inst].astype(jnp.float32)
            new_keys = fresh_all[: step + 1, 0, inst].astype(jnp.float32)
            new_values = fresh_all[: step + 1, 1, inst].astype(jnp.float32)
            cached = jnp.einsum("rkgd,rtkd->rkgt", query, keys) * scale
            cached = jnp.where(valid[:, None, None, :], cached, -1e30)
            recent = jnp.einsum("rkgd,srkd->rkgs", query, new_keys) * scale
            scores = jnp.concatenate([cached, recent], axis=-1)
            top = jnp.max(scores, axis=-1, keepdims=True)
            expo = jnp.exp(scores - top)
            probs = (expo / jnp.sum(expo, axis=-1, keepdims=True)).astype(jnp.bfloat16).astype(jnp.float32)
            context = jnp.einsum("rkgt,rtkd->rkgd", probs[..., :span], values)
            context = context + jnp.einsum("rkgs,srkd->rkgd", probs[..., span:], new_values)
            results.append(context.reshape(REQ, H * HD).astype(jnp.bfloat16))
        return jnp.stack(results)

    attention = lax.map(one, base)
    attention = jnp.transpose(attention, (1, 0, 2, 3)).reshape(STEPS * N_INST * REQ, H * HD)
    projected = jnp.dot(attention, out_weight, preferred_element_type=jnp.float32)
    return projected.astype(jnp.bfloat16).reshape(STEPS, N_INST * REQ, DW)
```

```python
import functools

import jax
import jax.numpy as jnp
from jax import lax
from jax.experimental import pallas as pl
from jax.experimental.pallas import tpu as pltpu
from jax.sharding import PartitionSpec as P

HD = 128
STEPS = 2
GROUP = 8
ROWS = STEPS * GROUP
PAGE = 16
BF = jnp.bfloat16
F32 = jnp.float32
NEG = -1e30
LOG2E = 1.4426950408889634
VMEM_LIMIT = 56 * 1024 * 1024


def pick_row(block, index):
    rows = lax.broadcasted_iota(jnp.int32, block.shape, 0)
    return jnp.sum(jnp.where(rows == index, block.astype(F32), 0.0), axis=0, keepdims=True)


def pack_kernel(mig, q_ref, kv_ref, out_ref, acc):
    mig_count = mig.shape[0]
    acc[...] = jnp.zeros_like(acc)
    for m in range(mig_count):
        for s in range(STEPS):
            row = pick_row(q_ref[s], mig[m])
            for g in range(GROUP):
                at = m * ROWS + s * GROUP + g
                acc[at : at + 1, :] = row[:, g * HD : (g + 1) * HD]
            for t in range(2):
                at = mig_count * ROWS + (m * STEPS + s) * 2 + t
                acc[at : at + 1, :] = pick_row(kv_ref[s, t], mig[m])
    out_ref[...] = acc[...].astype(BF)


def attend_kernel(
    tables, lens, mig, q_ref, kv_ref, far_ref, pages_hbm, ctx_ref, away_ref,
    pages, qs, snew, probs_new, acc, sem,
):
    slots = lens.shape[0]
    mig_count = mig.shape[0]
    max_pages = tables.shape[0]
    span = max_pages * PAGE
    page_count = pages.shape[0]
    parts = 8
    size = page_count // parts
    copies = [
        pltpu.make_async_copy(
            pages_hbm.at[pl.ds(i * size, size)], pages.at[pl.ds(i * size, size)], sem.at[i]
        )
        for i in range(parts)
    ]
    for copy in copies:
        copy.start()
    for s in range(STEPS):
        for g in range(GROUP):
            qs[pl.ds(s * GROUP + g, slots, stride=ROWS), :] = q_ref[
                s, :, g * HD : (g + 1) * HD
            ].astype(F32)
    far = far_ref[...].astype(F32)
    for m in range(mig_count):
        qs[pl.ds(pl.multiple_of(mig[m] * ROWS, ROWS), ROWS), :] = far[m * ROWS : (m + 1) * ROWS]
    slot_rows = lax.broadcasted_iota(jnp.int32, (slots, HD), 0)
    fresh = []
    for t in range(2):
        parts_t = []
        for s in range(STEPS):
            x = kv_ref[s, t].astype(F32)
            for m in range(mig_count):
                at = mig_count * ROWS + (m * STEPS + s) * 2 + t
                x = jnp.where(slot_rows == mig[m], far[at : at + 1], x)
            parts_t.append(x)
        fresh.append(jnp.concatenate(parts_t, axis=0).astype(BF))
    new_keys, new_values = fresh
    coef = LOG2E / HD**0.5
    contract_last = (((1,), (1,)), ((), ()))
    snew[...] = lax.dot_general(
        qs[...].astype(BF), new_keys, contract_last, preferred_element_type=F32
    )
    for copy in copies:
        copy.wait()

    row_step = lax.broadcasted_iota(jnp.int32, (ROWS, STEPS * slots), 0) // GROUP
    col = lax.broadcasted_iota(jnp.int32, (ROWS, STEPS * slots), 1)
    col_step = col // slots
    col_slot = col % slots
    causal = col_step <= row_step
    token = lax.broadcasted_iota(jnp.int32, (ROWS, span), 1)
    unroll = 8

    def some(i, carry):
        for u in range(unroll):
            r = i * unroll + u
            at = pl.ds(pl.multiple_of(r * ROWS, ROWS), ROWS)
            ids = [tables[j, r] for j in range(max_pages)]
            keys = jnp.concatenate([pages[p, 0] for p in ids], axis=0)
            values = jnp.concatenate([pages[p, 1] for p in ids], axis=0)
            scores = lax.dot_general(
                qs[at, :].astype(BF), keys, contract_last, preferred_element_type=F32
            )
            scores = jnp.where(token < lens[r], scores * coef, NEG)
            recent = jnp.where(causal & (col_slot == r), snew[at, :] * coef, NEG)
            top = jnp.maximum(
                jnp.max(scores, axis=-1, keepdims=True), jnp.max(recent, axis=-1, keepdims=True)
            )
            expo = jnp.exp2(scores - top)
            expo_new = jnp.exp2(recent - top)
            total = jnp.sum(expo, axis=-1, keepdims=True) + jnp.sum(
                expo_new, axis=-1, keepdims=True
            )
            inverse = 1.0 / total
            acc[at, :] = inverse * jnp.dot(expo.astype(BF), values, preferred_element_type=F32)
            probs_new[at, :] = expo_new * inverse
        return carry

    lax.fori_loop(0, slots // unroll, some, 0)
    acc[...] += jnp.dot(probs_new[...].astype(BF), new_values, preferred_element_type=F32)
    for s in range(STEPS):
        for g in range(GROUP):
            ctx_ref[s, :, g * HD : (g + 1) * HD] = acc[
                pl.ds(s * GROUP + g, slots, stride=ROWS), :
            ].astype(BF)
    for m in range(mig_count):
        away_ref[m * ROWS : (m + 1) * ROWS, :] = acc[
            pl.ds(pl.multiple_of(mig[m] * ROWS, ROWS), ROWS), :
        ].astype(BF)


def project_kernel(mig, ctx_ref, back_ref, w_hbm, mine_ref, other_ref, weights, rows, sem):
    blocks, depth, width = weights.shape
    chips = blocks // 2
    here = lax.axis_index("tp")
    chip, core = here // 2, here % 2
    order = [(1 - core, k) for k in range(chips)] + [(core, k) for k in range(chips)]
    copies = []
    for i, (c, k) in enumerate(order):
        at = lax.rem(chip + k, chips) * 2 + c
        copies.append(
            pltpu.make_async_copy(
                w_hbm.at[:, pl.ds(pl.multiple_of(at * width, width), width)],
                weights.at[i],
                sem.at[i],
            )
        )
        copies[i].start()
    slots = ctx_ref.shape[1]
    back = back_ref[...].astype(F32)
    slot_rows = lax.broadcasted_iota(jnp.int32, (slots, HD), 0)
    for s in range(STEPS):
        for g in range(GROUP):
            x = ctx_ref[s, :, g * HD : (g + 1) * HD].astype(F32)
            for m in range(mig.shape[0]):
                at = m * ROWS + s * GROUP + g
                x = jnp.where(slot_rows == mig[m], back[at : at + 1], x)
            rows[s * slots : (s + 1) * slots, g * HD : (g + 1) * HD] = x.astype(BF)
    for i in range(blocks):
        copies[i].wait()
        out = jnp.dot(rows[...], weights[i], preferred_element_type=F32).astype(BF)
        if i < chips:
            other_ref[i] = out
        else:
            mine_ref[i - chips] = out


def vmem():
    return pl.BlockSpec(memory_space=pltpu.VMEM)


def smem():
    return pl.BlockSpec(memory_space=pltpu.SMEM)


def hbm():
    return pl.BlockSpec(memory_space=pl.ANY)


def params():
    return pltpu.CompilerParams(vmem_limit_bytes=VMEM_LIMIT)


def pack(mig, queries, new_kv):
    rows = mig.shape[0] * (ROWS + 2 * STEPS)
    rows += -rows % 16
    return pl.pallas_call(
        pack_kernel,
        out_shape=jax.ShapeDtypeStruct((rows, HD), BF),
        in_specs=[smem(), vmem(), vmem()],
        out_specs=vmem(),
        scratch_shapes=[pltpu.VMEM((rows, HD), F32)],
        compiler_params=params(),
    )(mig, queries, new_kv)


def attend(tables, lens, mig, queries, new_kv, far, pages):
    slots = lens.shape[0]
    return pl.pallas_call(
        attend_kernel,
        out_shape=(
            jax.ShapeDtypeStruct(queries.shape, BF),
            jax.ShapeDtypeStruct((mig.shape[0] * ROWS, HD), BF),
        ),
        in_specs=[smem(), smem(), smem(), vmem(), vmem(), vmem(), hbm()],
        out_specs=(vmem(), vmem()),
        scratch_shapes=[
            pltpu.VMEM(pages.shape, BF),
            pltpu.VMEM((slots * ROWS, HD), F32),
            pltpu.VMEM((slots * ROWS, STEPS * slots), F32),
            pltpu.VMEM((slots * ROWS, STEPS * slots), F32),
            pltpu.VMEM((slots * ROWS, HD), F32),
            pltpu.SemaphoreType.DMA((8,)),
        ],
        compiler_params=params(),
    )(tables, lens, mig, queries, new_kv, far, pages)


def project(mig, ctx, back, weight, tp):
    depth, columns = weight.shape
    width = columns // tp
    rows = ctx.shape[0] * ctx.shape[1]
    half = jax.ShapeDtypeStruct((tp // 2, rows, width), BF)
    return pl.pallas_call(
        project_kernel,
        out_shape=(half, half),
        in_specs=[smem(), vmem(), vmem(), hbm()],
        out_specs=(vmem(), vmem()),
        scratch_shapes=[
            pltpu.VMEM((tp, depth, width), BF),
            pltpu.VMEM((rows, depth), BF),
            pltpu.SemaphoreType.DMA((tp,)),
        ],
        compiler_params=params(),
    )(mig, ctx, back, weight)


def swap_pairs(x, partner):
    count = partner.shape[0]
    here = lax.axis_index("inst")
    branches = [
        functools.partial(lax.ppermute, axis_name="inst", perm=[(i, i ^ c) for i in range(count)])
        for c in range(1, count)
    ]
    return lax.switch((here ^ partner[here]) - 1, branches, x)


def scatter_sum(mine, other, tp):
    chips = tp // 2
    got = lax.ppermute(other, "tp", [(i, i ^ 1) for i in range(tp)])
    pair = mine.astype(F32) + got.astype(F32)
    sent = pair.astype(BF)
    total = pair[0]
    for k in range(1, chips):
        shift = [(i, (i + 2 * k) % tp) for i in range(tp)]
        total = total + lax.ppermute(sent[k], "tp", shift).astype(F32)
    return total.astype(BF)


def body(tp, queries, new_kv, kv_pages, block_tables, lengths, migrating, partner, out_weight):
    steps, slots, _ = queries.shape
    far = swap_pairs(pack(migrating, queries, new_kv), partner)
    ctx, away = attend(block_tables.T, lengths, migrating, queries, new_kv, far, kv_pages)
    back = swap_pairs(away, partner)
    mine, other = project(migrating, ctx, back, out_weight, tp)
    out = scatter_sum(mine, other, tp)
    return out.reshape(steps, slots, out.shape[-1])


def solution(mesh):
    return jax.shard_map(
        functools.partial(body, mesh.shape["tp"]),
        mesh=mesh,
        in_specs=(
            P(None, "inst", "tp"),
            P(None, None, "inst", "tp"),
            P("inst", None, None, "tp"),
            P("inst", None),
            P("inst"),
            P("inst"),
            P(),
            P("tp", None),
        ),
        out_specs=P(None, "inst", "tp"),
        check_vma=False,
    )
```

```python
import functools

import jax
import jax.numpy as jnp
from jax import lax
from jax.experimental import pallas as pl
from jax.experimental.pallas import tpu as pltpu
from jax.sharding import PartitionSpec as P

HD = 128
STEPS = 2
GROUP = 8
ROWS = STEPS * GROUP
PAGE = 16
BF = jnp.bfloat16
F32 = jnp.float32
NEG = -1e30
LOG2E = 1.4426950408889634
VMEM_LIMIT = 20 * 1024 * 1024


def pick_row(block, index):
    rows = lax.broadcasted_iota(jnp.int32, block.shape, 0)
    return jnp.sum(jnp.where(rows == index, block.astype(F32), 0.0), axis=0, keepdims=True)


def pack_kernel(mig, partner, q_ref, kv_ref, out_ref, branch, acc):
    mig_count = mig.shape[0]
    here = lax.axis_index("inst")
    branch[0] = (here ^ partner[here]) - 1
    acc[...] = jnp.zeros_like(acc)
    for m in range(mig_count):
        for s in range(STEPS):
            row = pick_row(q_ref[s], mig[m])
            for g in range(GROUP):
                at = m * ROWS + s * GROUP + g
                acc[at : at + 1, :] = row[:, g * HD : (g + 1) * HD]
            for t in range(2):
                at = mig_count * ROWS + (m * STEPS + s) * 2 + t
                acc[at : at + 1, :] = pick_row(kv_ref[s, t], mig[m])
    out_ref[...] = acc[...].astype(BF)


def attend_kernel(
    tables, lens, mig, q_ref, kv_ref, far_ref, pages, ctx_ref, away_ref,
    qs, new_keys, new_values, acc,
):
    slots = lens.shape[0]
    mig_count = mig.shape[0]
    max_pages = tables.shape[0]
    span = max_pages * PAGE
    for s in range(STEPS):
        for g in range(GROUP):
            qs[pl.ds(s * GROUP + g, slots, stride=ROWS), :] = q_ref[
                s, :, g * HD : (g + 1) * HD
            ].astype(F32)
    far = far_ref[...].astype(F32)
    for m in range(mig_count):
        qs[pl.ds(pl.multiple_of(mig[m] * ROWS, ROWS), ROWS), :] = far[m * ROWS : (m + 1) * ROWS]
    slot_rows = lax.broadcasted_iota(jnp.int32, (slots, HD), 0)
    for t, out in enumerate((new_keys, new_values)):
        for s in range(STEPS):
            x = kv_ref[s, t].astype(F32)
            for m in range(mig_count):
                at = mig_count * ROWS + (m * STEPS + s) * 2 + t
                x = jnp.where(slot_rows == mig[m], far[at : at + 1], x)
            out[s] = x
    coef = LOG2E / HD**0.5
    batch = HD // ROWS
    lane = lax.broadcasted_iota(jnp.int32, (HD, HD), 1)
    lane_slot = lane // ROWS
    fresh_row = lax.broadcasted_iota(jnp.int32, (STEPS * batch, HD), 0)
    fresh_lane = lax.broadcasted_iota(jnp.int32, (STEPS * batch, HD), 1)
    fresh_valid = (fresh_row % batch == fresh_lane // ROWS) & (
        fresh_row // batch <= fresh_lane % ROWS // GROUP
    )
    token = lax.broadcasted_iota(jnp.int32, (span, HD), 0)
    one_row = lax.broadcasted_iota(jnp.int32, (1, HD), 1) // ROWS

    def some(i, carry):
        first = i * batch
        at = pl.ds(pl.multiple_of(first * ROWS, HD), HD)
        turned = qs[at, :].T
        ids = [[tables[j, first + u] for j in range(max_pages)] for u in range(batch)]
        keys = jnp.concatenate(
            [jnp.concatenate([pages[p, 0] for p in row], axis=0) for row in ids], axis=1
        )
        blocks = jnp.concatenate(
            [jnp.where(lane_slot == u, turned, 0.0).astype(BF) for u in range(batch)], axis=0
        )
        scores = jnp.dot(keys, blocks, preferred_element_type=F32)
        limit = jnp.zeros((1, HD), jnp.int32)
        for u in range(batch):
            limit = jnp.where(one_row == u, lens[first + u], limit)
        scores = jnp.where(token < limit, scores * coef, NEG)
        group = pl.ds(pl.multiple_of(first, batch), batch)
        near_keys = jnp.concatenate([new_keys[s, group, :] for s in range(STEPS)], axis=0)
        recent = jnp.dot(near_keys.astype(BF), turned.astype(BF), preferred_element_type=F32)
        recent = jnp.where(fresh_valid, recent * coef, NEG)
        top = jnp.maximum(
            jnp.max(scores, axis=0, keepdims=True), jnp.max(recent, axis=0, keepdims=True)
        )
        expo = jnp.exp2(scores - top)
        expo_new = jnp.exp2(recent - top)
        total = jnp.sum(expo, axis=0, keepdims=True) + jnp.sum(expo_new, axis=0, keepdims=True)
        inverse = 1.0 / total
        probs = (expo * inverse).T.astype(BF)
        pad = jnp.zeros((HD - STEPS * batch, HD), F32)
        probs_new = jnp.concatenate([expo_new * inverse, pad], axis=0).T.astype(BF)
        near_values = jnp.concatenate([new_values[s, group, :] for s in range(STEPS)] + [pad], axis=0)
        out = jnp.dot(probs_new, near_values.astype(BF), preferred_element_type=F32)
        old = []
        for u in range(batch):
            values = jnp.concatenate([pages[p, 1] for p in ids[u]], axis=0)
            old.append(
                jnp.dot(probs[u * ROWS : (u + 1) * ROWS], values, preferred_element_type=F32)
            )
        acc[at, :] = out + jnp.concatenate(old, axis=0)
        return carry

    lax.fori_loop(0, slots // batch, some, 0)
    for s in range(STEPS):
        for g in range(GROUP):
            ctx_ref[s, :, g * HD : (g + 1) * HD] = acc[
                pl.ds(s * GROUP + g, slots, stride=ROWS), :
            ].astype(BF)
    for m in range(mig_count):
        away_ref[m * ROWS : (m + 1) * ROWS, :] = acc[
            pl.ds(pl.multiple_of(mig[m] * ROWS, ROWS), ROWS), :
        ].astype(BF)
    rest = away_ref.shape[0] - mig_count * ROWS
    away_ref[mig_count * ROWS :, :] = jnp.zeros((rest, HD), BF)


def project_kernel(mig, ctx_ref, back_ref, weight, mine_ref, other_ref, rows):
    chips, _, width = mine_ref.shape
    here = lax.axis_index("tp")
    chip, core = here // 2, here % 2
    slots = ctx_ref.shape[1]
    back = back_ref[...].astype(F32)
    slot_rows = lax.broadcasted_iota(jnp.int32, (slots, HD), 0)
    for s in range(STEPS):
        for g in range(GROUP):
            x = ctx_ref[s, :, g * HD : (g + 1) * HD].astype(F32)
            for m in range(mig.shape[0]):
                at = m * ROWS + s * GROUP + g
                x = jnp.where(slot_rows == mig[m], back[at : at + 1], x)
            rows[s * slots : (s + 1) * slots, g * HD : (g + 1) * HD] = x.astype(BF)
    for c, out in ((1 - core, other_ref), (core, mine_ref)):
        for k in range(chips):
            at = lax.rem(chip + k, chips) * 2 + c
            block = weight[:, pl.ds(pl.multiple_of(at * width, width), width)]
            out[k] = jnp.dot(rows[...], block, preferred_element_type=F32).astype(BF)


def vmem():
    return pl.BlockSpec(memory_space=pltpu.VMEM)


def smem():
    return pl.BlockSpec(memory_space=pltpu.SMEM)


def params():
    return pltpu.CompilerParams(vmem_limit_bytes=VMEM_LIMIT)


def pack(mig, partner, queries, new_kv):
    rows = mig.shape[0] * (ROWS + 2 * STEPS)
    rows += -rows % 16
    return pl.pallas_call(
        pack_kernel,
        out_shape=(jax.ShapeDtypeStruct((rows, HD), BF), jax.ShapeDtypeStruct((1,), jnp.int32)),
        in_specs=[smem(), smem(), vmem(), vmem()],
        out_specs=(vmem(), smem()),
        scratch_shapes=[pltpu.VMEM((rows, HD), F32)],
        compiler_params=params(),
    )(mig, partner, queries, new_kv)


def attend(tables, lens, mig, queries, new_kv, far, pages):
    slots = lens.shape[0]
    return pl.pallas_call(
        attend_kernel,
        out_shape=(
            jax.ShapeDtypeStruct(queries.shape, BF),
            jax.ShapeDtypeStruct(far.shape, BF),
        ),
        in_specs=[smem(), smem(), smem(), vmem(), vmem(), vmem(), vmem()],
        out_specs=(vmem(), vmem()),
        scratch_shapes=[
            pltpu.VMEM((slots * ROWS, HD), F32),
            pltpu.VMEM((STEPS, slots, HD), F32),
            pltpu.VMEM((STEPS, slots, HD), F32),
            pltpu.VMEM((slots * ROWS, HD), F32),
        ],
        compiler_params=params(),
    )(tables, lens, mig, queries, new_kv, far, pages)


def project(mig, ctx, back, weight, tp):
    depth, columns = weight.shape
    width = columns // tp
    rows = ctx.shape[0] * ctx.shape[1]
    half = jax.ShapeDtypeStruct((tp // 2, rows, width), BF)
    return pl.pallas_call(
        project_kernel,
        out_shape=(half, half),
        in_specs=[smem(), vmem(), vmem(), vmem()],
        out_specs=(vmem(), vmem()),
        scratch_shapes=[pltpu.VMEM((rows, depth), BF)],
        compiler_params=params(),
    )(mig, ctx, back, weight)


def swap_pairs(x, branch, count):
    branches = [
        functools.partial(lax.ppermute, axis_name="inst", perm=[(i, i ^ c) for i in range(count)])
        for c in range(1, count)
    ]
    return lax.switch(branch, branches, x)


def scatter_sum(mine, other, tp):
    chips = tp // 2
    got = lax.ppermute(other, "tp", [(i, i ^ 1) for i in range(tp)])
    pair = mine.astype(F32) + got.astype(F32)
    sent = pair.astype(BF)
    total = pair[0]
    for k in range(1, chips):
        shift = [(i, (i + 2 * k) % tp) for i in range(tp)]
        total = total + lax.ppermute(sent[k], "tp", shift).astype(F32)
    return total.astype(BF)


def body(tp, queries, new_kv, kv_pages, block_tables, lengths, migrating, partner, out_weight):
    steps, slots, _ = queries.shape
    count = partner.shape[0]
    payload, branch = pack(migrating, partner, queries, new_kv)

    def exchange(turn, carry):
        payload, ctx = carry
        got = swap_pairs(payload, branch[0], count)

        def first(got):
            new_ctx, away = attend(
                block_tables.T, lengths, migrating, queries, new_kv, got, kv_pages
            )
            return away, new_ctx

        return lax.cond(turn == 0, first, lambda got: (got, ctx), got)

    turns = 2 + jnp.minimum(branch[0], 0)
    back, ctx = lax.fori_loop(0, turns, exchange, (payload, queries))
    mine, other = project(migrating, ctx, back, out_weight, tp)
    out = scatter_sum(mine, other, tp)
    return out.reshape(steps, slots, out.shape[-1])


def solution(mesh):
    return jax.shard_map(
        functools.partial(body, mesh.shape["tp"]),
        mesh=mesh,
        in_specs=(
            P(None, "inst", "tp"),
            P(None, None, "inst", "tp"),
            P("inst", None, None, "tp"),
            P("inst", None),
            P("inst"),
            P("inst"),
            P(),
            P("tp", None),
        ),
        out_specs=P(None, "inst", "tp"),
        check_vma=False,
    )
```

```python
import functools

import jax
import jax.numpy as jnp
from jax import lax
from jax.experimental import pallas as pl
from jax.experimental.pallas import tpu as pltpu
from jax.sharding import PartitionSpec as P

HD = 128
STEPS = 2
GROUP = 8
ROWS = STEPS * GROUP
BATCH = HD // ROWS
PAGE = 16
BF = jnp.bfloat16
F32 = jnp.float32
NEG = -1e30
COEF = 1.4426950408889634 / HD**0.5
SCORE_PARTS = 2
VALUE_PARTS = 2
MIB = 1024 * 1024
PACK_MIB = 56
P_MIB = 50


def pack_kernel(
    tables, lens, mig, partner, q_ref, kv_ref, pages,
    leave_ref, branch, turned_ref, turned_far, near_ref, qs, fresh, far, sem,
):
    slots = lens.shape[0]
    count = mig.shape[0]
    max_pages = tables.shape[0]
    copies = []
    for m in range(count):
        for j in range(max_pages):
            copies.append(
                pltpu.make_async_copy(
                    pages.at[tables[j, mig[m]]], leave_ref.at[m * max_pages + j], sem
                )
            )
    for copy in copies:
        copy.start()
    here = lax.axis_index("inst")
    branch[0] = (here ^ partner[here]) - 1
    half = lax.broadcasted_iota(jnp.int32, (2, PAGE, HD), 0)
    known = jnp.zeros((2, PAGE, HD), F32)
    for m in range(count):
        known = jnp.where(half == m, lens[mig[m]].astype(F32), known)
    leave_ref[count * max_pages] = known.astype(BF)
    for s in range(STEPS):
        for g in range(GROUP):
            qs[pl.ds(s * GROUP + g, slots, stride=ROWS), :] = q_ref[
                s, :, g * HD : (g + 1) * HD
            ].astype(F32)
    groups = slots // BATCH
    far[...] = jnp.zeros_like(far)
    for m in range(count):
        far[m * ROWS : (m + 1) * ROWS, :] = qs[
            pl.ds(pl.multiple_of(mig[m] * ROWS, ROWS), ROWS), :
        ]

    def turn(i, carry):
        turned_ref[i] = qs[pl.ds(pl.multiple_of(i * HD, HD), HD), :].T
        return carry

    lax.fori_loop(0, groups, turn, 0)
    turned_far[...] = far[...].T
    for s in range(STEPS):
        for t in range(2):
            fresh[s, t] = kv_ref[s, t].astype(F32)
            for i in range(groups):
                near_ref[i, t, s * BATCH : (s + 1) * BATCH, :] = fresh[
                    s, t, i * BATCH : (i + 1) * BATCH, :
                ]
            near_ref[groups, t, s * BATCH : (s + 1) * BATCH, :] = jnp.zeros((BATCH, HD), F32)
            for m in range(count):
                near_ref[groups, t, s * BATCH + m : s * BATCH + m + 1, :] = fresh[
                    s, t, pl.ds(mig[m], 1), :
                ]
    for copy in copies:
        copy.wait()


def add_new(probs_new, near_values):
    pad = jnp.zeros((HD - STEPS * BATCH, HD), F32)
    turned = jnp.concatenate([probs_new, pad], axis=0).T.astype(BF)
    values = jnp.concatenate([near_values, pad], axis=0).astype(BF)
    return jnp.dot(turned, values, preferred_element_type=F32)


def soft_group(
    page, limit, turned, near_keys, used, scores, probs, out, new_out, at, score_parts, parts
):
    max_pages = scores.shape[0] * HD // (PAGE * HD)
    lane_slot = lax.broadcasted_iota(jnp.int32, (HD, HD), 1) // ROWS
    score_size, size = used // score_parts, used // parts

    def product(h):
        slots = [h * score_size + u for u in range(score_size)]
        keys = jnp.concatenate(
            [
                jnp.concatenate([page(u, j, 0) for j in range(max_pages)], axis=0)
                for u in slots
            ],
            axis=1,
        )
        blocks = jnp.concatenate(
            [jnp.where(lane_slot == u, turned, 0.0).astype(BF) for u in slots], axis=0
        )
        return jnp.dot(keys, blocks, preferred_element_type=F32)

    if score_parts == 1:
        scores[...] = product(0)
    else:
        scores[...] = jnp.zeros_like(scores)

        def more(h, carry):
            scores[...] += product(h)
            return carry

        lax.fori_loop(0, score_parts, more, 0)

    row = lax.broadcasted_iota(jnp.int32, (STEPS * BATCH, HD), 0)
    lane = lax.broadcasted_iota(jnp.int32, (STEPS * BATCH, HD), 1)
    valid = (row % BATCH == lane // ROWS) & (row // BATCH <= lane % ROWS // GROUP)
    recent = jnp.dot(near_keys.astype(BF), turned.astype(BF), preferred_element_type=F32)
    recent = jnp.where(valid, recent * COEF, NEG)
    token = lax.broadcasted_iota(jnp.int32, (HD, HD), 0)
    chunks = scores.shape[0] // HD

    def rows_of(c):
        return pl.ds(pl.multiple_of(c * HD, HD), HD)

    def mask(c, top):
        x = jnp.where(token + c * HD < limit, scores[rows_of(c), :] * COEF, NEG)
        scores[rows_of(c), :] = x
        return jnp.maximum(top, jnp.max(x, axis=0, keepdims=True))

    top = lax.fori_loop(0, chunks, mask, jnp.max(recent, axis=0, keepdims=True))
    expo_new = jnp.exp2(recent - top)

    def power(c, total):
        x = jnp.exp2(scores[rows_of(c), :] - top)
        scores[rows_of(c), :] = x
        return total + jnp.sum(x, axis=0, keepdims=True)

    total = lax.fori_loop(0, chunks, power, jnp.sum(expo_new, axis=0, keepdims=True))
    inverse = 1.0 / total

    def divide(c, carry):
        probs[c] = (scores[rows_of(c), :] * inverse).T.astype(BF)
        return carry

    lax.fori_loop(0, chunks, divide, 0)
    new_out[at] = expo_new * inverse

    def weigh(h, carry):
        for v in range(size):
            u = h * size + v
            own = pl.ds(pl.multiple_of(u * ROWS, ROWS), ROWS)
            weight = jnp.concatenate([probs[c, own, :] for c in range(chunks)], axis=1)
            values = jnp.concatenate([page(u, j, 1) for j in range(max_pages)], axis=0)
            out[at, own, :] = jnp.dot(weight, values, preferred_element_type=F32)
        return carry

    lax.fori_loop(0, parts, weigh, 0)


def attend_kernel(tables, lens, turned_ref, near_ref, pages, out_ref, new_ref, scores, probs):
    slots = lens.shape[0]
    lane_slot = lax.broadcasted_iota(jnp.int32, (1, HD), 1) // ROWS

    def some(i, carry):
        first = i * BATCH
        limit = jnp.zeros((1, HD), jnp.int32)
        for u in range(BATCH):
            limit = jnp.where(lane_slot == u, lens[first + u], limit)

        def page(u, j, t):
            return pages[tables[j, first + u], t]

        soft_group(
            page, limit, turned_ref[i], near_ref[i, 0], BATCH,
            scores, probs, out_ref, new_ref, i, SCORE_PARTS, VALUE_PARTS,
        )
        return carry

    lax.fori_loop(0, slots // BATCH, some, 0)


def project_kernel(
    mig, near_ctx, near_new, turned_far, near_ref, come, weight_hbm, mine_ref, other_ref,
    weight, rows, scores, probs, full, far, far_new, sem,
):
    chips, _, width = mine_ref.shape
    here = lax.axis_index("tp")
    chip, core = here // 2, here % 2
    copies = []
    for c in (1 - core, core):
        for k in range(chips):
            i = len(copies)
            at = pl.multiple_of((lax.rem(chip + k, chips) * 2 + c) * width, width)
            copies.append(
                pltpu.make_async_copy(weight_hbm.at[:, pl.ds(at, width)], weight.at[i], sem.at[i])
            )
            copies[i].start()
    count = mig.shape[0]
    max_pages = come.shape[0] // count
    last = near_ref.shape[0] - 1
    lane_slot = lax.broadcasted_iota(jnp.int32, (1, HD), 1) // ROWS
    known = come[count * max_pages].astype(F32)
    limit = jnp.zeros((1, HD), F32)
    for m in range(count):
        limit = jnp.where(lane_slot == m, known[m, 0:1, :], limit)

    def page(u, j, t):
        return come[u * max_pages + j, t]

    soft_group(
        page, limit.astype(jnp.int32), turned_far[...], near_ref[last, 0],
        count, scores, probs, far, far_new, 0, 1, 1,
    )
    far[0, 0 : count * ROWS, :] += add_new(far_new[0], near_ref[last, 1])[0 : count * ROWS]
    for i in range(near_ctx.shape[0]):
        full[i] = near_ctx[i] + add_new(near_new[i], near_ref[i, 1])
    slots = near_ctx.shape[0] * BATCH
    slot_rows = lax.broadcasted_iota(jnp.int32, (slots, HD), 0)
    for s in range(STEPS):
        for g in range(GROUP):
            x = jnp.concatenate(
                [
                    full[i, pl.ds(s * GROUP + g, BATCH, stride=ROWS), :]
                    for i in range(slots // BATCH)
                ],
                axis=0,
            )
            for m in range(count):
                at = m * ROWS + s * GROUP + g
                x = jnp.where(slot_rows == mig[m], far[0, at : at + 1, :], x)
            rows[s * slots : (s + 1) * slots, g * HD : (g + 1) * HD] = x.astype(BF)
    for i, copy in enumerate(copies):
        copy.wait()
        out = other_ref if i < chips else mine_ref
        out[i % chips] = jnp.dot(rows[...], weight[i], preferred_element_type=F32).astype(BF)


def vmem():
    return pl.BlockSpec(memory_space=pltpu.VMEM)


def smem():
    return pl.BlockSpec(memory_space=pltpu.SMEM)


def params(mib):
    return pltpu.CompilerParams(vmem_limit_bytes=mib * MIB)


def pack(tables, lens, mig, partner, queries, new_kv, pages):
    slots = lens.shape[0]
    groups = slots // BATCH + 1
    return pl.pallas_call(
        pack_kernel,
        out_shape=(
            jax.ShapeDtypeStruct((mig.shape[0] * tables.shape[0] + 1, *pages.shape[1:]), BF),
            jax.ShapeDtypeStruct((1,), jnp.int32),
            jax.ShapeDtypeStruct((groups - 1, HD, HD), F32),
            jax.ShapeDtypeStruct((HD, HD), F32),
            jax.ShapeDtypeStruct((groups, 2, STEPS * BATCH, HD), F32),
        ),
        in_specs=[smem()] * 4 + [vmem()] * 2 + [pl.BlockSpec(memory_space=pl.ANY)],
        out_specs=(vmem(), smem(), vmem(), vmem(), vmem()),
        scratch_shapes=[
            pltpu.VMEM((slots * ROWS, HD), F32),
            pltpu.VMEM((STEPS, 2, slots, HD), F32),
            pltpu.VMEM((HD, HD), F32),
            pltpu.SemaphoreType.DMA,
        ],
        compiler_params=params(PACK_MIB),
    )(tables, lens, mig, partner, queries, new_kv, pages)


def soft_scratch(span):
    return [pltpu.VMEM((span, HD), F32), pltpu.VMEM((span // HD, HD, HD), BF)]


def attend(tables, lens, turned, near, pages):
    span = tables.shape[0] * PAGE
    rows = lens.shape[0] * ROWS
    return pl.pallas_call(
        attend_kernel,
        out_shape=(
            jax.ShapeDtypeStruct(turned.shape, F32),
            jax.ShapeDtypeStruct((turned.shape[0], STEPS * BATCH, HD), F32),
        ),
        in_specs=[smem()] * 2 + [vmem()] * 3,
        out_specs=(vmem(), vmem()),
        scratch_shapes=soft_scratch(span),
        compiler_params=params(20),
        cost_estimate=pl.CostEstimate(
            flops=rows * span * HD * 4, bytes_accessed=pages.size * 2, transcendentals=rows * span
        ),
    )(tables, lens, turned, near, pages)


def project(mig, near_ctx, near_new, turned, near, come, weight, tp):
    depth, columns = weight.shape
    rows = near_ctx.shape[0] * BATCH * STEPS
    span = come.shape[0] // mig.shape[0] * PAGE
    half = jax.ShapeDtypeStruct((tp // 2, rows, columns // tp), BF)
    return pl.pallas_call(
        project_kernel,
        out_shape=(half, half),
        in_specs=[smem()] + [vmem()] * 5 + [pl.BlockSpec(memory_space=pl.ANY)],
        out_specs=(vmem(), vmem()),
        scratch_shapes=[
            pltpu.VMEM((tp, depth, columns // tp), BF),
            pltpu.VMEM((rows, depth), BF),
            *soft_scratch(span),
            pltpu.VMEM(near_ctx.shape, F32),
            pltpu.VMEM((1, HD, HD), F32),
            pltpu.VMEM((1, STEPS * BATCH, HD), F32),
            pltpu.SemaphoreType.DMA((tp,)),
        ],
        compiler_params=params(P_MIB),
    )(mig, near_ctx, near_new, turned, near, come, weight)


def scatter_sum(mine, other, tp):
    chips = tp // 2
    got = lax.ppermute(other, "tp", [(i, i ^ 1) for i in range(tp)])
    pair = mine.astype(F32) + got.astype(F32)
    sent = pair.astype(BF)
    total = pair[0]
    for k in range(1, chips):
        shift = [(i, (i + 2 * k) % tp) for i in range(tp)]
        total = total + lax.ppermute(sent[k], "tp", shift).astype(F32)
    return total.astype(BF)


def swap_beside(leave, branch, count, beside, args):
    def one(c):
        pairs = [(i, i ^ c) for i in range(count)]
        return lambda leave, *args: (lax.ppermute(leave, "inst", pairs), beside(*args))

    return lax.switch(branch, [one(c) for c in range(1, count)], leave, *args)


def body(tp, queries, new_kv, kv_pages, block_tables, lengths, migrating, partner, out_weight):
    steps, slots, _ = queries.shape
    tables = block_tables.T
    leave, branch, turned, turned_far, near = pack(
        tables, lengths, migrating, partner, queries, new_kv, kv_pages
    )

    def turn(_, carry):
        leave, turned, _ = carry
        come, (ctx, new) = swap_beside(
            leave, branch[0], partner.shape[0], attend, (tables, lengths, turned, near, kv_pages)
        )
        return come, ctx, new

    turns = 1 + jnp.minimum(branch[0], 0)
    come, near_ctx, near_new = lax.fori_loop(0, turns, turn, (leave, turned, near[:-1, 0]))
    mine, other = project(migrating, near_ctx, near_new, turned_far, near, come, out_weight, tp)
    out = scatter_sum(mine, other, tp)
    return out.reshape(steps, slots, out.shape[-1])


def solution(mesh):
    return jax.shard_map(
        functools.partial(body, mesh.shape["tp"]),
        mesh=mesh,
        in_specs=(
            P(None, "inst", "tp"),
            P(None, None, "inst", "tp"),
            P("inst", None, None, "tp"),
            P("inst", None),
            P("inst"),
            P("inst"),
            P(),
            P("tp", None),
        ),
        out_specs=P(None, "inst", "tp"),
        check_vma=False,
    )
```

```python
import functools

import jax
import jax.numpy as jnp
from jax import lax
from jax.experimental import pallas as pl
from jax.experimental.pallas import tpu as pltpu
from jax.sharding import PartitionSpec as P

HD = 128
STEPS = 2
GROUP = 8
ROWS = STEPS * GROUP
BATCH = HD // ROWS
PAGE = 16
BF = jnp.bfloat16
F32 = jnp.float32
NEG = -1e30
COEF = 1.4426950408889634 / HD**0.5
SCORE_PARTS = 2
VALUE_PARTS = 2
MIB = 1024 * 1024
PACK_MIB = 56
A_MIB = 50
P_MIB = 50


def pack_kernel(
    tables, lens, mig, partner, q_ref, kv_ref, pages,
    leave_ref, branch, turned_ref, turned_far, keys_ref, near_ref, qs, fresh, far, sem,
):
    slots = lens.shape[0]
    count = mig.shape[0]
    max_pages = tables.shape[0]
    copies = []
    for m in range(count):
        for j in range(max_pages):
            copies.append(
                pltpu.make_async_copy(
                    pages.at[tables[j, mig[m]]], leave_ref.at[m * max_pages + j], sem
                )
            )
    for copy in copies:
        copy.start()
    here = lax.axis_index("inst")
    branch[0] = (here ^ partner[here]) - 1
    half = lax.broadcasted_iota(jnp.int32, (2, PAGE, HD), 0)
    known = jnp.zeros((2, PAGE, HD), F32)
    for m in range(count):
        known = jnp.where(half == m, lens[mig[m]].astype(F32), known)
    leave_ref[count * max_pages] = known.astype(BF)
    for s in range(STEPS):
        for g in range(GROUP):
            qs[pl.ds(s * GROUP + g, slots, stride=ROWS), :] = q_ref[
                s, :, g * HD : (g + 1) * HD
            ].astype(F32)
    groups = slots // BATCH
    far[...] = jnp.zeros_like(far)
    for m in range(count):
        far[m * ROWS : (m + 1) * ROWS, :] = qs[
            pl.ds(pl.multiple_of(mig[m] * ROWS, ROWS), ROWS), :
        ]

    def turn(i, carry):
        turned_ref[i] = qs[pl.ds(pl.multiple_of(i * HD, HD), HD), :].T
        return carry

    lax.fori_loop(0, groups, turn, 0)
    turned_far[...] = far[...].T
    keys_ref[...] = jnp.zeros_like(keys_ref)
    for s in range(STEPS):
        for t in range(2):
            fresh[s, t] = kv_ref[s, t].astype(F32)
            for i in range(groups):
                own = fresh[s, t, i * BATCH : (i + 1) * BATCH, :]
                near_ref[i, t, s * BATCH : (s + 1) * BATCH, :] = own
                if t == 0:
                    keys_ref[i, s * BATCH : (s + 1) * BATCH, :] = own
            near_ref[groups, t, s * BATCH : (s + 1) * BATCH, :] = jnp.zeros((BATCH, HD), F32)
            for m in range(count):
                near_ref[groups, t, s * BATCH + m : s * BATCH + m + 1, :] = fresh[
                    s, t, pl.ds(mig[m], 1), :
                ]
    for copy in copies:
        copy.wait()


def finish(context, new, near_values):
    used = STEPS * BATCH
    rows = jnp.concatenate([new, jnp.zeros((HD - new.shape[0], HD), F32)], axis=0).T
    values = jnp.concatenate([near_values, jnp.zeros((HD - used, HD), F32)], axis=0)
    new_context = jnp.dot(rows.astype(BF), values.astype(BF), preferred_element_type=F32)
    return (context + new_context) * rows[:, used : used + 1]


def soft_group(
    page, limit, turned, near_keys, used, scores, probs, out, new_out, at, score_parts, parts,
    values_here=None,
):
    max_pages = scores.shape[0] * HD // (PAGE * HD)
    lane_slot = lax.broadcasted_iota(jnp.int32, (HD, HD), 1) // ROWS
    score_size, size = used // score_parts, used // parts

    def product(h):
        slots = [h * score_size + u for u in range(score_size)]
        keys = jnp.concatenate(
            [
                jnp.concatenate([page(u, j, 0) for j in range(max_pages)], axis=0)
                for u in slots
            ],
            axis=1,
        )
        blocks = jnp.concatenate(
            [jnp.where(lane_slot == u, turned, 0.0).astype(BF) for u in slots], axis=0
        )
        return jnp.dot(keys, blocks, preferred_element_type=F32)

    if score_parts == 1:
        scores[...] = product(0)
    else:
        scores[...] = jnp.zeros_like(scores)

        def more(h, carry):
            scores[...] += product(h)
            return carry

        lax.fori_loop(0, score_parts, more, 0)

    row = lax.broadcasted_iota(jnp.int32, (STEPS * BATCH, HD), 0)
    lane = lax.broadcasted_iota(jnp.int32, (STEPS * BATCH, HD), 1)
    valid = (row % BATCH == lane // ROWS) & (row // BATCH <= lane % ROWS // GROUP)
    recent = jnp.dot(near_keys.astype(BF), turned.astype(BF), preferred_element_type=F32)
    recent = jnp.where(valid, recent * COEF, NEG)
    token = lax.broadcasted_iota(jnp.int32, (HD, HD), 0)
    chunks = scores.shape[0] // HD

    def rows_of(c):
        return pl.ds(pl.multiple_of(c * HD, HD), HD)

    def mask(c, top):
        x = jnp.where(token + c * HD < limit, scores[rows_of(c), :] * COEF, NEG)
        scores[rows_of(c), :] = x
        return jnp.maximum(top, jnp.max(x, axis=0, keepdims=True))

    top = lax.fori_loop(0, chunks, mask, jnp.max(recent, axis=0, keepdims=True))
    expo_new = jnp.exp2(recent - top)

    def power(c, total):
        x = jnp.exp2(scores[rows_of(c), :] - top)
        probs[c] = x.T.astype(BF)
        return total + jnp.sum(x, axis=0, keepdims=True)

    total = lax.fori_loop(0, chunks, power, jnp.sum(expo_new, axis=0, keepdims=True))
    new_out[at, 0 : STEPS * BATCH, :] = expo_new
    new_out[at, STEPS * BATCH :, :] = jnp.broadcast_to(1.0 / total, (BATCH, HD))

    if values_here is not None:
        values_here()

    def weigh(h, carry):
        for v in range(size):
            u = h * size + v
            own = pl.ds(pl.multiple_of(u * ROWS, ROWS), ROWS)
            weight = jnp.concatenate([probs[c, own, :] for c in range(chunks)], axis=1)
            values = jnp.concatenate([page(u, j, 1) for j in range(max_pages)], axis=0)
            out[at, own, :] = jnp.dot(weight, values, preferred_element_type=F32)
        return carry

    lax.fori_loop(0, parts, weigh, 0)


def attend_kernel(
    tables, lens, turned_ref, keys_ref, pages, out_ref, new_ref, held, scores, probs, sem
):
    chunks = sem.shape[1]
    size = pages.shape[0] // chunks
    copies = []
    for t in range(2):
        for c in range(chunks):
            part = pl.ds(c * size, size)
            copies.append(pltpu.make_async_copy(pages.at[part, t], held.at[t, part], sem.at[t, c]))
    for copy in copies:
        copy.start()
    for copy in copies[:chunks]:
        copy.wait()
    slots = lens.shape[0]
    lane_slot = lax.broadcasted_iota(jnp.int32, (1, HD), 1) // ROWS

    def some(i, carry):
        first = i * BATCH
        limit = jnp.zeros((1, HD), jnp.int32)
        for u in range(BATCH):
            limit = jnp.where(lane_slot == u, lens[first + u], limit)

        def page(u, j, t):
            return held[t, tables[j, first + u]]

        def values_here():
            @pl.when(i == 0)
            def _():
                for copy in copies[chunks:]:
                    copy.wait()

        soft_group(
            page, limit, turned_ref[i], keys_ref[i, 0 : STEPS * BATCH, :], BATCH,
            scores, probs, out_ref, new_ref, i, SCORE_PARTS, VALUE_PARTS, values_here,
        )
        return carry

    lax.fori_loop(0, slots // BATCH, some, 0)


def project_kernel(
    mig, near_ctx, near_new, turned_far, near_ref, come, weight_hbm, mine_ref, other_ref,
    weight, rows, scores, probs, full, far, far_new, sem,
):
    chips, _, width = mine_ref.shape
    here = lax.axis_index("tp")
    chip, core = here // 2, here % 2
    copies = []
    for c in (1 - core, core):
        for k in range(chips):
            i = len(copies)
            ahead = (0, 1 + 2 * c, 3 - 2 * c, 2)[k]
            at = pl.multiple_of((lax.rem(chip + ahead, chips) * 2 + c) * width, width)
            copies.append(
                pltpu.make_async_copy(weight_hbm.at[:, pl.ds(at, width)], weight.at[i], sem.at[i])
            )
            copies[i].start()
    count = mig.shape[0]
    max_pages = come.shape[0] // count
    last = near_ref.shape[0] - 1
    lane_slot = lax.broadcasted_iota(jnp.int32, (1, HD), 1) // ROWS
    known = come[count * max_pages].astype(F32)
    limit = jnp.zeros((1, HD), F32)
    for m in range(count):
        limit = jnp.where(lane_slot == m, known[m, 0:1, :], limit)

    def page(u, j, t):
        return come[u * max_pages + j, t]

    far[...] = jnp.zeros_like(far)
    soft_group(
        page, limit.astype(jnp.int32), turned_far[...], near_ref[last, 0],
        count, scores, probs, far, far_new, 0, 1, 1,
    )
    far[0] = finish(far[0], far_new[0], near_ref[last, 1])
    for i in range(near_ctx.shape[0]):
        full[i] = finish(near_ctx[i], near_new[i], near_ref[i, 1])
    slots = near_ctx.shape[0] * BATCH
    slot_rows = lax.broadcasted_iota(jnp.int32, (slots, HD), 0)
    for s in range(STEPS):
        for g in range(GROUP):
            x = jnp.concatenate(
                [
                    full[i, pl.ds(s * GROUP + g, BATCH, stride=ROWS), :]
                    for i in range(slots // BATCH)
                ],
                axis=0,
            )
            for m in range(count):
                at = m * ROWS + s * GROUP + g
                x = jnp.where(slot_rows == mig[m], far[0, at : at + 1, :], x)
            rows[s * slots : (s + 1) * slots, g * HD : (g + 1) * HD] = x.astype(BF)
    for i, copy in enumerate(copies):
        copy.wait()
        out = other_ref if i < chips else mine_ref
        out[i % chips] = jnp.dot(rows[...], weight[i], preferred_element_type=F32).astype(BF)


def vmem():
    return pl.BlockSpec(memory_space=pltpu.VMEM)


def smem():
    return pl.BlockSpec(memory_space=pltpu.SMEM)


def params(mib):
    return pltpu.CompilerParams(vmem_limit_bytes=mib * MIB)


def pack(tables, lens, mig, partner, queries, new_kv, pages):
    slots = lens.shape[0]
    groups = slots // BATCH + 1
    return pl.pallas_call(
        pack_kernel,
        out_shape=(
            jax.ShapeDtypeStruct((mig.shape[0] * tables.shape[0] + 1, *pages.shape[1:]), BF),
            jax.ShapeDtypeStruct((1,), jnp.int32),
            jax.ShapeDtypeStruct((groups - 1, HD, HD), F32),
            jax.ShapeDtypeStruct((HD, HD), F32),
            jax.ShapeDtypeStruct((groups - 1, (STEPS + 1) * BATCH, HD), F32),
            jax.ShapeDtypeStruct((groups, 2, STEPS * BATCH, HD), F32),
        ),
        in_specs=[smem()] * 4 + [vmem()] * 2 + [pl.BlockSpec(memory_space=pl.ANY)],
        out_specs=(vmem(), smem(), vmem(), vmem(), vmem(), vmem()),
        scratch_shapes=[
            pltpu.VMEM((slots * ROWS, HD), F32),
            pltpu.VMEM((STEPS, 2, slots, HD), F32),
            pltpu.VMEM((HD, HD), F32),
            pltpu.SemaphoreType.DMA,
        ],
        compiler_params=params(PACK_MIB),
    )(tables, lens, mig, partner, queries, new_kv, pages)


def soft_scratch(span):
    return [pltpu.VMEM((span, HD), F32), pltpu.VMEM((span // HD, HD, HD), BF)]


def attend(tables, lens, turned, keys, pages):
    span = tables.shape[0] * PAGE
    rows = lens.shape[0] * ROWS
    count, kinds = pages.shape[:2]
    return pl.pallas_call(
        attend_kernel,
        out_shape=(
            jax.ShapeDtypeStruct(turned.shape, F32),
            jax.ShapeDtypeStruct(keys.shape, F32),
        ),
        in_specs=[smem()] * 2 + [vmem()] * 2 + [pl.BlockSpec(memory_space=pl.ANY)],
        out_specs=(vmem(), vmem()),
        scratch_shapes=[
            pltpu.VMEM((kinds, count, *pages.shape[2:]), BF),
            *soft_scratch(span),
            pltpu.SemaphoreType.DMA((kinds, 4)),
        ],
        compiler_params=params(A_MIB),
        cost_estimate=pl.CostEstimate(
            flops=rows * span * HD * 4, bytes_accessed=pages.size * 2, transcendentals=rows * span
        ),
    )(tables, lens, turned, keys, pages)


def project(mig, near_ctx, near_new, turned, near, come, weight, tp):
    depth, columns = weight.shape
    rows = near_ctx.shape[0] * BATCH * STEPS
    span = come.shape[0] // mig.shape[0] * PAGE
    half = jax.ShapeDtypeStruct((tp // 2, rows, columns // tp), BF)
    return pl.pallas_call(
        project_kernel,
        out_shape=(half, half),
        in_specs=[smem()] + [vmem()] * 5 + [pl.BlockSpec(memory_space=pl.ANY)],
        out_specs=(vmem(), vmem()),
        scratch_shapes=[
            pltpu.VMEM((tp, depth, columns // tp), BF),
            pltpu.VMEM((rows, depth), BF),
            *soft_scratch(span),
            pltpu.VMEM(near_ctx.shape, F32),
            pltpu.VMEM((1, HD, HD), F32),
            pltpu.VMEM((1, (STEPS + 1) * BATCH, HD), F32),
            pltpu.SemaphoreType.DMA((tp,)),
        ],
        compiler_params=params(P_MIB),
    )(mig, near_ctx, near_new, turned, near, come, weight)


def scatter_sum(mine, other, tp):
    def ahead(up, down):
        return [(i, (i + 2 * (down if i % 2 else up)) % tp) for i in range(tp)]

    got = lax.ppermute(other, "tp", [(i, i ^ 1) for i in range(tp)])
    pair = mine.astype(F32) + got.astype(F32)
    sent = pair.astype(BF)
    total = pair[0]
    for k, pairs in enumerate((ahead(1, -1), ahead(-1, 1), ahead(2, 2)), 1):
        total = total + lax.ppermute(sent[k], "tp", pairs).astype(F32)
    return total.astype(BF)


def swap_beside(leave, branch, count, beside, args):
    def one(c):
        pairs = [(i, i ^ c) for i in range(count)]
        return lambda leave, *args: (lax.ppermute(leave, "inst", pairs), beside(*args))

    return lax.switch(branch, [one(c) for c in range(1, count)], leave, *args)


def body(tp, queries, new_kv, kv_pages, block_tables, lengths, migrating, partner, out_weight):
    steps, slots, _ = queries.shape
    tables = block_tables.T
    leave, branch, turned, turned_far, keys, near = pack(
        tables, lengths, migrating, partner, queries, new_kv, kv_pages
    )

    def turn(_, carry):
        leave, turned, keys = carry
        come, (ctx, new) = swap_beside(
            leave, branch[0], partner.shape[0], attend, (tables, lengths, turned, keys, kv_pages)
        )
        return come, ctx, new

    turns = 1 + jnp.minimum(lax.axis_index("inst"), 0)
    come, near_ctx, near_new = lax.fori_loop(0, turns, turn, (leave, turned, keys))
    mine, other = project(migrating, near_ctx, near_new, turned_far, near, come, out_weight, tp)
    out = scatter_sum(mine, other, tp)
    return out.reshape(steps, slots, out.shape[-1])


def solution(mesh):
    return jax.shard_map(
        functools.partial(body, mesh.shape["tp"]),
        mesh=mesh,
        in_specs=(
            P(None, "inst", "tp"),
            P(None, None, "inst", "tp"),
            P("inst", None, None, "tp"),
            P("inst", None),
            P("inst"),
            P("inst"),
            P(),
            P("tp", None),
        ),
        out_specs=P(None, "inst", "tp"),
        check_vma=False,
    )
```

```python
import functools

import jax
import jax.numpy as jnp
from jax import lax
from jax.experimental import pallas as pl
from jax.experimental.pallas import tpu as pltpu
from jax.sharding import PartitionSpec as P

HD = 128
STEPS = 2
GROUP = 8
ROWS = STEPS * GROUP
BATCH = HD // ROWS
PAGE = 16
BF = jnp.bfloat16
F32 = jnp.float32
NEG = -1e30
COEF = 1.4426950408889634 / HD**0.5
SCORE_PARTS = 2
VALUE_PARTS = 2
MIB = 1024 * 1024
PACK_MIB = 56
A_MIB = 50
P_MIB = 50


def pack_kernel(
    tables, lens, mig, partner, q_ref, kv_ref, pages,
    leave_ref, branch, turned_ref, turned_far, keys_ref, near_ref, qs, fresh, far, sem,
):
    slots = lens.shape[0]
    count = mig.shape[0]
    max_pages = tables.shape[0]
    copies = []
    for m in range(count):
        for j in range(max_pages):
            copies.append(
                pltpu.make_async_copy(
                    pages.at[tables[j, mig[m]]], leave_ref.at[m * max_pages + j], sem
                )
            )
    for copy in copies:
        copy.start()
    here = lax.axis_index("inst")
    branch[0] = (here ^ partner[here]) - 1
    half = lax.broadcasted_iota(jnp.int32, (2, PAGE, HD), 0)
    known = jnp.zeros((2, PAGE, HD), F32)
    for m in range(count):
        known = jnp.where(half == m, lens[mig[m]].astype(F32), known)
    leave_ref[count * max_pages] = known.astype(BF)
    for s in range(STEPS):
        for g in range(GROUP):
            qs[pl.ds(s * GROUP + g, slots, stride=ROWS), :] = q_ref[
                s, :, g * HD : (g + 1) * HD
            ].astype(F32)
    groups = slots // BATCH
    far[...] = jnp.zeros_like(far)
    for m in range(count):
        far[m * ROWS : (m + 1) * ROWS, :] = qs[
            pl.ds(pl.multiple_of(mig[m] * ROWS, ROWS), ROWS), :
        ]

    def turn(i, carry):
        turned_ref[i] = qs[pl.ds(pl.multiple_of(i * HD, HD), HD), :].T
        return carry

    lax.fori_loop(0, groups, turn, 0)
    turned_far[...] = far[...].T
    keys_ref[...] = jnp.zeros_like(keys_ref)
    for s in range(STEPS):
        for t in range(2):
            fresh[s, t] = kv_ref[s, t].astype(F32)
            for i in range(groups):
                own = fresh[s, t, i * BATCH : (i + 1) * BATCH, :]
                near_ref[i, t, s * BATCH : (s + 1) * BATCH, :] = own
                if t == 0:
                    keys_ref[i, s * BATCH : (s + 1) * BATCH, :] = own
            near_ref[groups, t, s * BATCH : (s + 1) * BATCH, :] = jnp.zeros((BATCH, HD), F32)
            for m in range(count):
                near_ref[groups, t, s * BATCH + m : s * BATCH + m + 1, :] = fresh[
                    s, t, pl.ds(mig[m], 1), :
                ]
    for copy in copies:
        copy.wait()


def finish(context, new, near_values):
    used = STEPS * BATCH
    rows = jnp.concatenate([new, jnp.zeros((HD - new.shape[0], HD), F32)], axis=0).T
    values = jnp.concatenate([near_values, jnp.zeros((HD - used, HD), F32)], axis=0)
    new_context = jnp.dot(rows.astype(BF), values.astype(BF), preferred_element_type=F32)
    return (context + new_context) * rows[:, used : used + 1]


def soft_group(
    page, limit, turned, near_keys, used, scores, probs, out, new_out, at, score_parts, parts,
    values_here=None,
):
    max_pages = scores.shape[0] * HD // (PAGE * HD)
    lane_slot = lax.broadcasted_iota(jnp.int32, (HD, HD), 1) // ROWS
    score_size, size = used // score_parts, used // parts

    def product(h):
        slots = [h * score_size + u for u in range(score_size)]
        keys = jnp.concatenate(
            [
                jnp.concatenate([page(u, j, 0) for j in range(max_pages)], axis=0)
                for u in slots
            ],
            axis=1,
        )
        blocks = jnp.concatenate(
            [jnp.where(lane_slot == u, turned, 0.0).astype(BF) for u in slots], axis=0
        )
        return jnp.dot(keys, blocks, preferred_element_type=F32)

    if score_parts == 1:
        scores[...] = product(0)
    else:
        scores[...] = jnp.zeros_like(scores)

        def more(h, carry):
            scores[...] += product(h)
            return carry

        lax.fori_loop(0, score_parts, more, 0)

    row = lax.broadcasted_iota(jnp.int32, (STEPS * BATCH, HD), 0)
    lane = lax.broadcasted_iota(jnp.int32, (STEPS * BATCH, HD), 1)
    valid = (row % BATCH == lane // ROWS) & (row // BATCH <= lane % ROWS // GROUP)
    recent = jnp.dot(near_keys.astype(BF), turned.astype(BF), preferred_element_type=F32)
    recent = jnp.where(valid, recent * COEF, NEG)
    token = lax.broadcasted_iota(jnp.int32, (HD, HD), 0)
    chunks = scores.shape[0] // HD

    def rows_of(c):
        return pl.ds(pl.multiple_of(c * HD, HD), HD)

    def mask(c, top):
        x = jnp.where(token + c * HD < limit, scores[rows_of(c), :] * COEF, NEG)
        scores[rows_of(c), :] = x
        return jnp.maximum(top, jnp.max(x, axis=0, keepdims=True))

    top = lax.fori_loop(0, chunks, mask, jnp.max(recent, axis=0, keepdims=True))
    expo_new = jnp.exp2(recent - top)

    def power(c, total):
        x = jnp.exp2(scores[rows_of(c), :] - top)
        probs[c] = x.T.astype(BF)
        return total + jnp.sum(x, axis=0, keepdims=True)

    total = lax.fori_loop(0, chunks, power, jnp.sum(expo_new, axis=0, keepdims=True))
    new_out[at, 0 : STEPS * BATCH, :] = expo_new
    new_out[at, STEPS * BATCH :, :] = jnp.broadcast_to(1.0 / total, (BATCH, HD))

    if values_here is not None:
        values_here()

    def weigh(h, carry):
        for v in range(size):
            u = h * size + v
            own = pl.ds(pl.multiple_of(u * ROWS, ROWS), ROWS)
            weight = jnp.concatenate([probs[c, own, :] for c in range(chunks)], axis=1)
            values = jnp.concatenate([page(u, j, 1) for j in range(max_pages)], axis=0)
            out[at, own, :] = jnp.dot(weight, values, preferred_element_type=F32)
        return carry

    lax.fori_loop(0, parts, weigh, 0)


def attend_kernel(
    tables, lens, turned_ref, keys_ref, pages, out_ref, new_ref, held, scores, probs, sem
):
    chunks = sem.shape[1]
    size = pages.shape[0] // chunks
    copies = []
    for t in range(2):
        for c in range(chunks):
            part = pl.ds(c * size, size)
            copies.append(pltpu.make_async_copy(pages.at[part, t], held.at[t, part], sem.at[t, c]))
    for copy in copies:
        copy.start()
    for copy in copies[:chunks]:
        copy.wait()
    slots = lens.shape[0]
    lane_slot = lax.broadcasted_iota(jnp.int32, (1, HD), 1) // ROWS

    def some(i, carry):
        first = i * BATCH
        limit = jnp.zeros((1, HD), jnp.int32)
        for u in range(BATCH):
            limit = jnp.where(lane_slot == u, lens[first + u], limit)

        def page(u, j, t):
            return held[t, tables[j, first + u]]

        def values_here():
            @pl.when(i == 0)
            def _():
                for copy in copies[chunks:]:
                    copy.wait()

        soft_group(
            page, limit, turned_ref[i], keys_ref[i, 0 : STEPS * BATCH, :], BATCH,
            scores, probs, out_ref, new_ref, i, SCORE_PARTS, VALUE_PARTS, values_here,
        )
        return carry

    lax.fori_loop(0, slots // BATCH, some, 0)


def project_kernel(
    mig, near_ctx, near_new, turned_far, near_ref, come, weight_hbm, mine_ref, other_ref,
    weight, rows, scores, probs, full, far, far_new, sem,
):
    chips, _, width = mine_ref.shape
    here = lax.axis_index("tp")
    chip, core = here // 2, here % 2
    copies = []
    for c in (1 - core, core):
        for k in range(chips):
            i = len(copies)
            ahead = (0, 1 + 2 * c, 3 - 2 * c, 2)[k]
            at = pl.multiple_of((lax.rem(chip + ahead, chips) * 2 + c) * width, width)
            copies.append(
                pltpu.make_async_copy(weight_hbm.at[:, pl.ds(at, width)], weight.at[i], sem.at[i])
            )
            copies[i].start()
    count = mig.shape[0]
    max_pages = come.shape[0] // count
    last = near_ref.shape[0] - 1
    lane_slot = lax.broadcasted_iota(jnp.int32, (1, HD), 1) // ROWS
    known = come[count * max_pages].astype(F32)
    limit = jnp.zeros((1, HD), F32)
    for m in range(count):
        limit = jnp.where(lane_slot == m, known[m, 0:1, :], limit)

    def page(u, j, t):
        return come[u * max_pages + j, t]

    far[...] = jnp.zeros_like(far)
    soft_group(
        page, limit.astype(jnp.int32), turned_far[...], near_ref[last, 0],
        count, scores, probs, far, far_new, 0, 1, 1,
    )
    far[0] = finish(far[0], far_new[0], near_ref[last, 1])
    for i in range(near_ctx.shape[0]):
        full[i] = finish(near_ctx[i], near_new[i], near_ref[i, 1])
    slots = near_ctx.shape[0] * BATCH
    slot_rows = lax.broadcasted_iota(jnp.int32, (slots, HD), 0)
    for s in range(STEPS):
        for g in range(GROUP):
            x = jnp.concatenate(
                [
                    full[i, pl.ds(s * GROUP + g, BATCH, stride=ROWS), :]
                    for i in range(slots // BATCH)
                ],
                axis=0,
            )
            for m in range(count):
                at = m * ROWS + s * GROUP + g
                x = jnp.where(slot_rows == mig[m], far[0, at : at + 1, :], x)
            rows[s * slots : (s + 1) * slots, g * HD : (g + 1) * HD] = x.astype(BF)
    for i, copy in enumerate(copies):
        copy.wait()
        out = other_ref if i < chips else mine_ref
        out[i % chips] = jnp.dot(rows[...], weight[i], preferred_element_type=F32).astype(BF)


def vmem():
    return pl.BlockSpec(memory_space=pltpu.VMEM)


def smem():
    return pl.BlockSpec(memory_space=pltpu.SMEM)


def params(mib):
    return pltpu.CompilerParams(vmem_limit_bytes=mib * MIB)


def pack(tables, lens, mig, partner, queries, new_kv, pages):
    slots = lens.shape[0]
    groups = slots // BATCH + 1
    return pl.pallas_call(
        pack_kernel,
        out_shape=(
            jax.ShapeDtypeStruct((mig.shape[0] * tables.shape[0] + 1, *pages.shape[1:]), BF),
            jax.ShapeDtypeStruct((1,), jnp.int32),
            jax.ShapeDtypeStruct((groups - 1, HD, HD), F32),
            jax.ShapeDtypeStruct((HD, HD), F32),
            jax.ShapeDtypeStruct((groups - 1, (STEPS + 1) * BATCH, HD), F32),
            jax.ShapeDtypeStruct((groups, 2, STEPS * BATCH, HD), F32),
        ),
        in_specs=[smem()] * 4 + [vmem()] * 2 + [pl.BlockSpec(memory_space=pl.ANY)],
        out_specs=(vmem(), smem(), vmem(), vmem(), vmem(), vmem()),
        scratch_shapes=[
            pltpu.VMEM((slots * ROWS, HD), F32),
            pltpu.VMEM((STEPS, 2, slots, HD), F32),
            pltpu.VMEM((HD, HD), F32),
            pltpu.SemaphoreType.DMA,
        ],
        compiler_params=params(PACK_MIB),
    )(tables, lens, mig, partner, queries, new_kv, pages)


def soft_scratch(span):
    return [pltpu.VMEM((span, HD), F32), pltpu.VMEM((span // HD, HD, HD), BF)]


def attend(tables, lens, turned, keys, pages):
    span = tables.shape[0] * PAGE
    rows = lens.shape[0] * ROWS
    count, kinds = pages.shape[:2]
    return pl.pallas_call(
        attend_kernel,
        out_shape=(
            jax.ShapeDtypeStruct(turned.shape, F32),
            jax.ShapeDtypeStruct(keys.shape, F32),
        ),
        in_specs=[smem()] * 2 + [vmem()] * 2 + [pl.BlockSpec(memory_space=pl.ANY)],
        out_specs=(vmem(), vmem()),
        scratch_shapes=[
            pltpu.VMEM((kinds, count, *pages.shape[2:]), BF),
            *soft_scratch(span),
            pltpu.SemaphoreType.DMA((kinds, 1)),
        ],
        compiler_params=params(A_MIB),
        cost_estimate=pl.CostEstimate(
            flops=rows * span * HD * 4, bytes_accessed=pages.size * 2, transcendentals=rows * span
        ),
    )(tables, lens, turned, keys, pages)


def project(mig, near_ctx, near_new, turned, near, come, weight, tp):
    depth, columns = weight.shape
    rows = near_ctx.shape[0] * BATCH * STEPS
    span = come.shape[0] // mig.shape[0] * PAGE
    half = jax.ShapeDtypeStruct((tp // 2, rows, columns // tp), BF)
    return pl.pallas_call(
        project_kernel,
        out_shape=(half, half),
        in_specs=[smem()] + [vmem()] * 5 + [pl.BlockSpec(memory_space=pl.ANY)],
        out_specs=(vmem(), vmem()),
        scratch_shapes=[
            pltpu.VMEM((tp, depth, columns // tp), BF),
            pltpu.VMEM((rows, depth), BF),
            *soft_scratch(span),
            pltpu.VMEM(near_ctx.shape, F32),
            pltpu.VMEM((1, HD, HD), F32),
            pltpu.VMEM((1, (STEPS + 1) * BATCH, HD), F32),
            pltpu.SemaphoreType.DMA((tp,)),
        ],
        compiler_params=params(P_MIB),
    )(mig, near_ctx, near_new, turned, near, come, weight)


def scatter_sum(mine, other, tp):
    def ahead(up, down):
        return [(i, (i + 2 * (down if i % 2 else up)) % tp) for i in range(tp)]

    got = lax.ppermute(other, "tp", [(i, i ^ 1) for i in range(tp)])
    pair = mine.astype(F32) + got.astype(F32)
    sent = pair.astype(BF)
    total = pair[0]
    for k, pairs in enumerate((ahead(1, -1), ahead(-1, 1), ahead(2, 2)), 1):
        total = total + lax.ppermute(sent[k], "tp", pairs).astype(F32)
    return total.astype(BF)


def swap_beside(leave, branch, count, beside, args):
    def one(c):
        pairs = [(i, i ^ c) for i in range(count)]
        return lambda leave, *args: (lax.ppermute(leave, "inst", pairs), beside(*args))

    return lax.switch(branch, [one(c) for c in range(1, count)], leave, *args)


def body(tp, queries, new_kv, kv_pages, block_tables, lengths, migrating, partner, out_weight):
    steps, slots, _ = queries.shape
    tables = block_tables.T
    leave, branch, turned, turned_far, keys, near = pack(
        tables, lengths, migrating, partner, queries, new_kv, kv_pages
    )

    def turn(_, carry):
        leave, turned, keys = carry
        come, (ctx, new) = swap_beside(
            leave, branch[0], partner.shape[0], attend, (tables, lengths, turned, keys, kv_pages)
        )
        return come, ctx, new

    turns = 1 + jnp.minimum(lax.axis_index("inst"), 0)
    come, near_ctx, near_new = lax.fori_loop(0, turns, turn, (leave, turned, keys))
    mine, other = project(migrating, near_ctx, near_new, turned_far, near, come, out_weight, tp)
    out = scatter_sum(mine, other, tp)
    return out.reshape(steps, slots, out.shape[-1])


def solution(mesh):
    return jax.shard_map(
        functools.partial(body, mesh.shape["tp"]),
        mesh=mesh,
        in_specs=(
            P(None, "inst", "tp"),
            P(None, None, "inst", "tp"),
            P("inst", None, None, "tp"),
            P("inst", None),
            P("inst"),
            P("inst"),
            P(),
            P("tp", None),
        ),
        out_specs=P(None, "inst", "tp"),
        check_vma=False,
    )
```
